32 devices in a mesh: fsdp: 4 (over y, x), ctx: 4 (over z), tp: 2 (over core).
Axes of the slice: x: 2, y: 2, z: 4, core: 2. Of those that a mesh axis runs over, the one named last changes fastest.
Arguments:
- tokens: bfloat16 [4, 1024, 2048], P('fsdp', 'ctx'), may hold values from -8 to 8
- segments: int32 [4, 1024], P('fsdp', 'ctx'), may hold values from 0 to 974, as said below
- positions: int32 [4, 1024], P('fsdp', 'ctx'), may hold values from 0 to 768, as said below
- first_gain: float32 [2048], replicated, may hold values from 0.5 to 1.5
- first_shift: float32 [2048], replicated, may hold values from -1.8 to 1.8
- query_weight: bfloat16 [2048, 2048], P(('fsdp', 'ctx'), 'tp'), may hold values from -0.125 to 0.125
- query_bias: float32 [2048], replicated, may hold values from -3 to 3
- key_weight: bfloat16 [2048, 2048], P(('fsdp', 'ctx'), 'tp'), may hold values from -0.125 to 0.125
- key_bias: float32 [32, 16], replicated, may hold values from -4 to 4
- value_weight: bfloat16 [2048, 2048], P(('fsdp', 'ctx'), 'tp'), may hold values from -0.125 to 0.125
- value_bias: float32 [2048], replicated, may hold values from -3 to 3
- out_weight: bfloat16 [2048, 2048], P('tp', ('fsdp', 'ctx')), may hold values from -0.5 to 0.5
- second_gain: float32 [2048], replicated, may hold values from 0.5 to 1.5
- second_shift: float32 [2048], replicated, may hold values from -1.8 to 1.8
- gate_weight: bfloat16 [2048, 5632], P(('fsdp', 'ctx'), 'tp'), may hold values from -0.125 to 0.125
- up_weight: bfloat16 [2048, 5632], P(('fsdp', 'ctx'), 'tp'), may hold values from -0.125 to 0.125
- down_weight: bfloat16 [5632, 2048], P('tp', ('fsdp', 'ctx')), may hold values from -0.078125 to 0.078125
- cotangent: bfloat16 [4, 1024, 2048], P('fsdp', 'ctx'), may hold values from -6 to 6
Outputs:
- output: bfloat16 [4, 1024, 2048], P('fsdp', 'ctx')
- tokens_gradient: bfloat16 [4, 1024, 2048], P('fsdp', 'ctx')
- first_gain_gradient: float32 [2048], replicated
- first_shift_gradient: float32 [2048], replicated
- query_weight_gradient: float32 [2048, 2048], P(('fsdp', 'ctx'), 'tp')
- query_bias_gradient: float32 [2048], replicated
- key_weight_gradient: float32 [2048, 2048], P(('fsdp', 'ctx'), 'tp')
- key_bias_gradient: float32 [32, 16], replicated
- value_weight_gradient: float32 [2048, 2048], P(('fsdp', 'ctx'), 'tp')
- value_bias_gradient: float32 [2048], replicated
- out_weight_gradient: float32 [2048, 2048], P('tp', ('fsdp', 'ctx'))
- second_gain_gradient: float32 [2048], replicated
- second_shift_gradient: float32 [2048], replicated
- gate_weight_gradient: float32 [2048, 5632], P(('fsdp', 'ctx'), 'tp')
- up_weight_gradient: float32 [2048, 5632], P(('fsdp', 'ctx'), 'tp')
- down_weight_gradient: float32 [5632, 2048], P('tp', ('fsdp', 'ctx'))
The draws below stay inside these ranges and needn't reach their ends.
Inputs may be any that keep to these rules, and one draw needn't show every extreme that they name: `segments`: each token's segment number is the index, within its sequence, of the first token of its document; documents are contiguous runs of tokens. Every second sequence (which ones is drawn from the seed) has documents beginning only at tokens 0 and 255. In each of the other sequences the last document holds the last max(2, 50) tokens. `positions`: each token's position is its index within its sequence minus its segment number.
All inputs are finite; a program needn't handle non-finite values.
Results may differ from the reference program's by a relative error of at most 0.024.
Values may be sent and summed in bfloat16 or wider, within the bound.
No kernel may reach another device: no remote copies, remote signals or barrier semaphores. Data moves between devices by JAX's collectives and lax.ppermute only.
A program may use at most 320 MiB of HBM per device.

```python
import math
import jax
import jax.numpy as jnp
from jax import lax

D = 2048
HEADS = 32
HEAD = 64
ROT = 16
FF = 5632
SHARD_TOK = 256
LENGTH = 1024
SEQUENCES = 4


def document_starts(key):
    index = jnp.arange(LENGTH, dtype=jnp.int32)
    shortest = max(2, LENGTH * 200 // 4096)
    longest = max(shortest + 1, LENGTH * 2000 // 4096)
    count = LENGTH // shortest + 1
    gaps = jax.random.randint(jax.random.fold_in(key, 11), (SEQUENCES, count), shortest, longest + 1)
    starts = jnp.cumsum(gaps, axis=1).astype(jnp.int32) - gaps
    last_start = LENGTH - shortest
    starts = jnp.where(starts <= LENGTH - 2 * shortest, starts, last_start)
    starts = jnp.concatenate([starts, jnp.full((SEQUENCES, 1), last_start, jnp.int32)], axis=1)
    cut_marks = jnp.any(starts[:, None, :] == index[None, :, None], axis=2)
    flip = jax.random.randint(jax.random.fold_in(key, 12), (), 0, 2)
    whole = jnp.arange(SEQUENCES, dtype=jnp.int32) % 2 == flip
    whole_marks = (index[None, :] == 0) | (index[None, :] == SHARD_TOK - 1)
    marks = jnp.where(whole[:, None], whole_marks, cut_marks)
    return lax.cummax(jnp.where(marks, index[None, :], 0), axis=1).astype(jnp.int32)


def draw_segments(key, part):
    return document_starts(key)


def draw_positions(key, part):
    index = jnp.arange(LENGTH, dtype=jnp.int32)
    return (index[None, :] - document_starts(key)).astype(jnp.int32)


def draw_tokens(key, part):
    key = jax.random.fold_in(key, 5)
    keys = jax.random.split(key, 3)
    row_scale = jnp.exp(jax.random.uniform(keys[0], (SEQUENCES, LENGTH, 1), jnp.float32, math.log(0.3), math.log(3.0)))
    col_scale = jnp.exp(jax.random.uniform(keys[1], (D,), jnp.float32, math.log(0.3), math.log(3.0)))
    base = jax.random.normal(keys[2], (SEQUENCES, LENGTH, D), jnp.float32)
    return jnp.clip(base * row_scale * col_scale, -8.0, 8.0).astype(jnp.bfloat16)


def raised(result, key, source, target, shards_of, factor):
    def block_of(position):
        return (jnp.arange(result.shape[position]) // (result.shape[position] // shards_of)).reshape((-1,) + (1,) * (result.ndim - 1 - position))

    near = jax.random.permutation(key, shards_of)[block_of(target)]
    second = (block_of(target) + shards_of // 2) % shards_of
    return jnp.where((block_of(source) == near) | (block_of(source) == second), factor * result, result)


def steps_of(own_key, extent, cuts, smallest, top_value):
    factor_of, own = 1.0, jax.random.fold_in(own_key, 6)
    for position, shards_of in cuts:
        draws = jnp.exp(jax.random.uniform(jax.random.fold_in(own, position), (shards_of,), jnp.float32, smallest / len(cuts), top_value / len(cuts)))
        factor_of = factor_of * jnp.repeat(draws, extent[position] // shards_of).reshape([-1 if axis == position else 1 for axis in range(len(extent))])
    return factor_of


def bell_draw(rng, extent, deviation, limit, shards=(), kind=jnp.bfloat16):
    entries = deviation * jax.random.normal(rng, extent, jnp.float32)
    if shards:
        entries = entries * steps_of(rng, extent, shards, -0.22, 0.18)
    return jnp.clip(entries, -limit, limit).astype(kind)


def gaussian_with(rng, dims, deviation, limit, cuts, heavy, held_as=jnp.bfloat16):
    entries = deviation * jax.random.normal(rng, dims, jnp.float32)
    if cuts:
        entries = entries * steps_of(rng, dims, cuts, -0.22, 0.18)
    return jnp.clip(raised(entries, jax.random.fold_in(rng, 3), *heavy), -limit, limit).astype(held_as)


def setup_inputs(seed: int = 0) -> dict:
    splits = jax.random.split(jax.random.key(seed), 19)
    tokens = draw_tokens(jax.random.fold_in(splits[18], 71), 0)
    segments = draw_segments(jax.random.fold_in(splits[18], 71), 0)
    positions = draw_positions(jax.random.fold_in(splits[18], 71), 0)
    first_gain = jnp.clip(1.0 + 0.1 * jax.random.normal(splits[3], (D,), jnp.float32), 0.5, 1.5)
    first_shift = bell_draw(splits[4], (D,), 0.3, 1.8, (), jnp.float32)
    query_weight = bell_draw(splits[5], (D, D), D ** -0.5, 0.125, ((0, 16), (1, 2)))
    query_bias = bell_draw(splits[6], (D,), 0.5, 3.0, (), jnp.float32)
    key_weight = bell_draw(splits[7], (D, D), D ** -0.5, 0.125, ((0, 16), (1, 2)))
    key_bias = bell_draw(splits[8], (HEADS, ROT), 1.0, 4.0, (), jnp.float32)
    value_weight = bell_draw(splits[9], (D, D), D ** -0.5, 0.125, ((0, 16), (1, 2)))
    value_bias = bell_draw(splits[10], (D,), 0.5, 3.0, (), jnp.float32)
    out_weight = bell_draw(splits[11], (D, D), (D // 16) ** -0.5, 0.5, ((0, 2), (1, 16)))
    second_gain = jnp.clip(1.0 + 0.1 * jax.random.normal(splits[12], (D,), jnp.float32), 0.5, 1.5)
    second_shift = bell_draw(splits[13], (D,), 0.3, 1.8, (), jnp.float32)
    gate_weight = bell_draw(splits[14], (D, FF), D ** -0.5, 0.125, ((0, 16), (1, 2)))
    up_weight = bell_draw(splits[15], (D, FF), D ** -0.5, 0.125, ((0, 16), (1, 2)))
    down_weight = bell_draw(splits[16], (FF, D), FF ** -0.5, 0.078125, ((0, 2), (1, 16)))
    cotangent = gaussian_with(splits[17], (SEQUENCES, LENGTH, D), 1.0, 6.0, ((0, 4), (1, 4)), (1, 2, 4, 2.0))
    return dict(tokens=tokens, segments=segments, positions=positions, first_gain=first_gain, first_shift=first_shift, query_weight=query_weight, query_bias=query_bias, key_weight=key_weight, key_bias=key_bias, value_weight=value_weight, value_bias=value_bias, out_weight=out_weight, second_gain=second_gain, second_shift=second_shift, gate_weight=gate_weight, up_weight=up_weight, down_weight=down_weight, cotangent=cotangent)


NEG = -1e+30
EPS = 1e-05
HIGH = lax.Precision.HIGHEST

@jax.custom_vjp
def low(v):
    return lax.optimization_barrier(v.astype(jnp.bfloat16)).astype(jnp.float32)

@jax.custom_vjp
def low_back(v):
    return v

def low_keep(v):
    return (low(v), None)

def low_pass(kept, grad):
    return (grad,)

def back_keep(v):
    return (v, None)

def back_low(kept, grad):
    return (low(grad),)
low.defvjp(low_keep, low_pass)
low_back.defvjp(back_keep, back_low)

def norm_rows(values, gain, shift):
    mean = lax.optimization_barrier(jnp.mean(values, axis=-1, keepdims=True))
    centred = values - mean
    inverse = lax.rsqrt(lax.optimization_barrier(jnp.mean(centred * centred, axis=-1, keepdims=True)) + EPS)
    return centred * inverse * gain + shift

def rotary_tables(places, rotary):
    half = rotary // 2
    freqs = 1.0 / 10000.0 ** (jnp.arange(half, dtype=jnp.float32) * 2.0 / rotary)
    angle = places.astype(jnp.float32)[..., None] * freqs
    return (jnp.cos(angle)[..., None, :], jnp.sin(angle)[..., None, :])

def rotate(values, cosine, sine, rotary):
    half = rotary // 2
    first = values[..., :half]
    second = values[..., half:rotary]
    return jnp.concatenate([first * cosine - second * sine, second * cosine + first * sine, values[..., rotary:]], axis=-1)

def matmul(left, right):
    return jnp.dot(left, right, precision=HIGH)

def one_sequence(inputs, starts, places, params):
    first_gain, first_shift, query_weight, query_bias, key_weight, key_bias, value_weight, value_bias, out_weight, second_gain, second_shift, gate_weight, up_weight, down_weight = params
    normed = low(norm_rows(inputs, first_gain, first_shift))
    query = low_back(matmul(normed, query_weight) + query_bias).reshape(LENGTH, HEADS, HEAD)
    keys = low_back(matmul(normed, key_weight)).reshape(LENGTH, HEADS, HEAD)
    keys = jnp.concatenate([keys[..., :ROT] + key_bias, keys[..., ROT:]], axis=-1)
    values = low_back(low(matmul(normed, value_weight) + value_bias)).reshape(LENGTH, HEADS, HEAD)
    cosine, sine = rotary_tables(places, ROT)
    query = low_back(low(rotate(query, cosine, sine, ROT)))
    keys = low_back(low(rotate(keys, cosine, sine, ROT)))
    index = jnp.arange(LENGTH, dtype=jnp.int32)
    block = min(LENGTH, 512)
    score_scale = 1.0 / math.sqrt(HEAD)

    def attend(item):
        query_block, start_block, index_block = item
        scores = low_back(jnp.einsum('qhd,khd->hqk', query_block, keys, precision=HIGH) * score_scale)
        allowed = ((index[None, :] >= start_block[:, None]) & (index[None, :] <= index_block[:, None]))[None]
        masked = jnp.where(allowed, scores, NEG)
        log_total = jax.nn.logsumexp(masked, axis=-1, keepdims=True)
        probs = jnp.where(allowed, jnp.exp(masked - log_total), 0.0)
        return jnp.einsum('hqk,khd->qhd', low(probs), values, precision=HIGH)
    count = LENGTH // block
    attended = lax.map(jax.checkpoint(attend), (query.reshape(count, block, HEADS, HEAD), starts.reshape(count, block), index.reshape(count, block)))
    attended = low_back(low(attended.reshape(LENGTH, D)))
    mixed = inputs + low_back(matmul(attended, out_weight))
    normed2 = low(norm_rows(mixed, second_gain, second_shift))
    gate = low_back(matmul(normed2, gate_weight))
    upward = low_back(matmul(normed2, up_weight))
    activation = low(jax.nn.silu(gate) * upward)
    return mixed + low_back(matmul(activation, down_weight))

def reference(tokens, segments, positions, first_gain, first_shift, query_weight, query_bias, key_weight, key_bias, value_weight, value_bias, out_weight, second_gain, second_shift, gate_weight, up_weight, down_weight, cotangent):
    params = tuple((p.astype(jnp.float32) for p in (first_gain, first_shift, query_weight, query_bias, key_weight, key_bias, value_weight, value_bias, out_weight, second_gain, second_shift, gate_weight, up_weight, down_weight)))

    def forward(inputs, weights):

        def step(carry, item):
            return (carry, one_sequence(item[0], item[1], item[2], weights))
        return lax.scan(step, None, (inputs, segments, positions))[1]
    output, pullback = jax.vjp(forward, tokens.astype(jnp.float32), params)
    tokens_gradient, grads = pullback(cotangent.astype(jnp.float32))
    return (output.astype(jnp.bfloat16), tokens_gradient.astype(jnp.bfloat16), grads[0], grads[1], grads[2], grads[3], grads[4], grads[5], grads[6], grads[7], grads[8], grads[9], grads[10], grads[11], grads[12], grads[13])
```

```python
import math

import jax
import jax.numpy as jnp
from jax import lax
from jax.sharding import PartitionSpec as P

HEADS = 32
HEAD = 64


NEG = -1e30
EPS = 1e-05
BF = jnp.bfloat16
F32 = jnp.float32


def norm_parts(values, gain, shift):
    mean = jnp.mean(values, axis=-1, keepdims=True)
    centred = values - mean
    inverse = lax.rsqrt(jnp.mean(centred * centred, axis=-1, keepdims=True) + EPS)
    unit = centred * inverse
    return (unit * gain + shift, unit, inverse)


def norm_back(grad, unit, inverse, gain):
    scaled = grad * gain
    return inverse * (
        scaled
        - jnp.mean(scaled, axis=-1, keepdims=True)
        - unit * jnp.mean(scaled * unit, axis=-1, keepdims=True)
    )


def rotary_tables(places, rotary):
    half = rotary // 2
    freqs = 1.0 / 10000.0 ** (jnp.arange(half, dtype=jnp.float32) * 2.0 / rotary)
    angle = places.astype(jnp.float32)[..., None] * freqs
    return (jnp.cos(angle)[..., None, :], jnp.sin(angle)[..., None, :])


def rotate(values, cosine, sine, rotary):
    half = rotary // 2
    first = values[..., :half]
    second = values[..., half:rotary]
    return jnp.concatenate(
        [first * cosine - second * sine, second * cosine + first * sine, values[..., rotary:]],
        axis=-1,
    )


def rotate_back(grad, cosine, sine, rotary):
    half = rotary // 2
    first = grad[..., :half]
    second = grad[..., half:rotary]
    return jnp.concatenate(
        [first * cosine + second * sine, second * cosine - first * sine, grad[..., rotary:]],
        axis=-1,
    )


def rounded(values):
    return lax.optimization_barrier(values.astype(jnp.bfloat16)).astype(jnp.float32)


def dot(left, right, dims, out=F32):
    return lax.dot_general(left, right, ((dims[:1], dims[1:]), ((), ())), preferred_element_type=out)


def contract_rows(left, right, out=F32):
    return dot(left, right, (0, 0), out)


def times(left, right, out=F32):
    return dot(left, right, (1, 0), out)


def times_transposed(left, right, out=F32):
    return dot(left, right, (1, 1), out)


def shift(values, axis, step):
    size = lax.axis_size(axis)
    return lax.ppermute(values, axis, [(i, (i + step) % size) for i in range(size)])


def swap(values, axis, bit):
    size = lax.axis_size(axis)
    return lax.ppermute(values, axis, [(i, i ^ bit) for i in range(size)])


def take(blocks, index):
    return lax.dynamic_index_in_dim(blocks, index, 0, keepdims=False)


def stacked(pairs, count):
    first = pairs[0][1]
    out = jnp.zeros((count,) + first.shape, first.dtype)
    for index, block in pairs:
        out = lax.dynamic_update_index_in_dim(out, block, index, 0)
    return out


def line_gather(block, axis):
    size = lax.axis_size(axis)
    me = lax.axis_index(axis)
    pairs = [(me, block)]
    right = left = block
    for step in range(1, (size - 1) // 2 + 1):
        right = shift(right, axis, 1)
        left = shift(left, axis, -1)
        pairs += [((me - step) % size, right), ((me + step) % size, left)]
    if size % 2 == 0:
        half = block.shape[0] // 2
        far = jnp.concatenate([shift(right[:half], axis, 1), shift(left[half:], axis, -1)], 0)
        pairs.append(((me + size // 2) % size, far))
    return stacked(pairs, size)


def line_sum(blocks, axis):
    size = lax.axis_size(axis)
    me = lax.axis_index(axis)
    rows = blocks.shape[1]
    half = rows // 2
    right = left = None
    if size % 2 == 0:
        far = take(blocks, (me + size // 2) % size).astype(BF)
        right = shift(far[:half], axis, 1)
        left = shift(far[half:], axis, -1)
    for step in range((size - 1) // 2, 0, -1):
        ahead = take(blocks, (me + step) % size).astype(F32)
        behind = take(blocks, (me - step) % size).astype(F32)
        if right is not None:
            if right.shape[0] != rows:
                ahead = jnp.concatenate([ahead[:half] + right.astype(F32), ahead[half:]], 0)
                behind = jnp.concatenate([behind[:half], behind[half:] + left.astype(F32)], 0)
            else:
                ahead = ahead + right.astype(F32)
                behind = behind + left.astype(F32)
        right = shift(ahead.astype(BF), axis, 1)
        left = shift(behind.astype(BF), axis, -1)
    return take(blocks, me).astype(F32) + right.astype(F32) + left.astype(F32)


def line_exchange(blocks, axis):
    size = lax.axis_size(axis)
    me = lax.axis_index(axis)
    pairs = [(me, take(blocks, me))]
    steps = sorted(range(1, size), key=lambda step: (-min(step, size - step), step))
    for step in steps:
        pairs.append(((me - step) % size, shift(take(blocks, (me + step) % size), axis, step)))
    return stacked(pairs, size)


def plane_gather(block, axis):
    me = lax.axis_index(axis)
    half = block.shape[0] // 2
    near = swap(block, axis, 1)
    side = swap(block, axis, 2)
    low = swap(near[:half], axis, 2)
    high = swap(side[half:], axis, 1)
    far = jnp.concatenate([low, high], 0)
    return stacked([(me, block), (me ^ 1, near), (me ^ 2, side), (me ^ 3, far)], 4)


def plane_sum(blocks, axis):
    me = lax.axis_index(axis)
    far = blocks(me ^ 3).astype(BF)
    half = far.shape[0] // 2
    low = swap(far[:half], axis, 1)
    high = swap(far[half:], axis, 2)
    side = blocks(me ^ 2).astype(F32)
    near = blocks(me ^ 1).astype(F32)
    side = jnp.concatenate([side[:half] + low.astype(F32), side[half:]], 0).astype(BF)
    near = jnp.concatenate([near[:half], near[half:] + high.astype(F32)], 0).astype(BF)
    side = swap(side, axis, 2)
    near = swap(near, axis, 1)
    return blocks(me).astype(F32) + side.astype(F32) + near.astype(F32)


def total(values, axes):
    for axis in axes:
        bit = 1
        while bit < lax.axis_size(axis):
            values = values + swap(values, axis, bit)
            bit *= 2
    return values


def pair_rows(block, axis="tp"):
    me = lax.axis_index(axis)
    return stacked([(me, block), (1 - me, swap(block, axis, 1))], 2)


def gather_rows(block):
    lined = line_gather(block, "ctx")
    size, rows, width = lined.shape
    both = pair_rows(lined)
    return jnp.swapaxes(both, 0, 1).reshape(size * 2 * rows, width)


def scatter_rows(partial):
    size = lax.axis_size("ctx")
    me = lax.axis_index("tp")
    rows = partial.shape[0] // (2 * size)
    split = jnp.swapaxes(partial.reshape(size, 2, rows, partial.shape[1]), 0, 1)
    other = swap(take(split, 1 - me).astype(BF), "tp", 1)
    return line_sum(take(split, me).astype(F32) + other.astype(F32), "ctx")


def gather_weight(block):
    turned = line_exchange(jnp.swapaxes(block, 0, 1), "ctx")
    size, rows, columns = turned.shape
    return plane_gather(turned.reshape(size * rows, columns), "fsdp").reshape(-1, columns)


def scatter_gradient(rows_in, grads):
    size = lax.axis_size("ctx")
    width = rows_in.shape[1] // lax.axis_size("fsdp")

    def block(index):
        return contract_rows(lax.dynamic_slice_in_dim(rows_in, index * width, width, 1), grads)

    own = plane_sum(block, "fsdp").astype(BF)
    turned = line_exchange(own.reshape(size, width // size, -1), "ctx")
    return jnp.swapaxes(turned, 0, 1)


def on_device(
    tokens,
    segments,
    positions,
    first_gain,
    first_shift,
    query_weight,
    query_bias,
    key_weight,
    key_bias,
    value_weight,
    value_bias,
    out_weight,
    second_gain,
    second_shift,
    gate_weight,
    up_weight,
    down_weight,
    cotangent,
):
    local_rows, model_width = tokens.shape[1:]
    tensor_rank, tensor_size = lax.axis_index("tp"), lax.axis_size("tp")
    ctx_rank, ctx_size = lax.axis_index("ctx"), lax.axis_size("ctx")
    length = local_rows * ctx_size
    own_rows = local_rows // tensor_size
    heads = HEADS // (tensor_size * ctx_size)
    columns = heads * HEAD
    first_head = (tensor_rank * ctx_size + ctx_rank) * heads
    first_col = first_head * HEAD
    hidden = gate_weight.shape[1] // ctx_size
    rotary = key_bias.shape[1]
    score_scale = 1.0 / math.sqrt(HEAD)
    weight_rows = query_weight.shape[0]

    def split(weight):
        return weight.reshape(weight.shape[0], ctx_size, -1)

    own_tokens = lax.dynamic_slice_in_dim(tokens[0], tensor_rank * own_rows, own_rows, 0)
    own_cotangent = lax.dynamic_slice_in_dim(cotangent[0], tensor_rank * own_rows, own_rows, 0)
    inputs = own_tokens.astype(F32)
    normed1, unit1, inverse1 = norm_parts(inputs, first_gain, first_shift)
    projections = gather_weight(
        jnp.concatenate([split(query_weight), split(key_weight), split(value_weight)], 2)
    )
    normed1_all = gather_rows(normed1.astype(BF))
    starts = lax.all_gather(segments[0], "ctx", axis=0, tiled=True)
    out_all = gather_weight(split(out_weight.T))
    gate_up = gather_weight(jnp.concatenate([split(gate_weight), split(up_weight)], 2))
    down_all = gather_weight(split(down_weight.T))
    cotangent_all = gather_rows(own_cotangent)

    bias_query = lax.dynamic_slice_in_dim(query_bias, first_col, columns, 0)
    bias_value = lax.dynamic_slice_in_dim(value_bias, first_col, columns, 0)
    bias_key = lax.dynamic_slice_in_dim(key_bias, first_head, heads, 0)
    projected = times(normed1_all, projections)
    heads_shape = (length, heads, HEAD)
    query_pre = (projected[:, :columns] + bias_query).reshape(heads_shape)
    key_pre = projected[:, columns : 2 * columns].reshape(heads_shape)
    key_pre = jnp.concatenate([key_pre[..., :rotary] + bias_key, key_pre[..., rotary:]], axis=-1)
    value_low = (projected[:, 2 * columns :] + bias_value).astype(BF).reshape(heads_shape)
    index = jnp.arange(length, dtype=jnp.int32)
    cosine, sine = rotary_tables(index - starts, rotary)
    query_low = rotate(query_pre, cosine, sine, rotary).astype(BF)
    key_low = rotate(key_pre, cosine, sine, rotary).astype(BF)
    allowed = ((index[None, :] >= starts[:, None]) & (index[None, :] <= index[:, None]))[None]
    scores = jnp.einsum("qhd,khd->hqk", query_low, key_low, preferred_element_type=F32) * score_scale
    masked = jnp.where(allowed, scores, NEG)
    highest = jnp.max(masked, axis=-1, keepdims=True)
    weights = jnp.exp(masked - highest)
    sums = jnp.sum(weights, axis=-1, keepdims=True)
    log_total = highest + jnp.log(sums)
    attended = jnp.einsum("hqk,khd->qhd", weights.astype(BF), value_low, preferred_element_type=F32)
    attended = attended / jnp.swapaxes(sums, 0, 1)
    attended_low = attended.astype(BF).reshape(length, columns)

    mixed = inputs + scatter_rows(times_transposed(attended_low, out_all))
    normed2, unit2, inverse2 = norm_parts(mixed, second_gain, second_shift)
    normed2_all = gather_rows(normed2.astype(BF))

    gate_upward = times(normed2_all, gate_up)
    gate, upward = gate_upward[:, :hidden], gate_upward[:, hidden:]
    gate_sigmoid = jax.nn.sigmoid(gate)
    swish = gate * gate_sigmoid
    activation_low = (swish * upward).astype(BF)
    activation_grad = times(cotangent_all, down_all)
    gate_grad_low = (
        activation_grad * upward * gate_sigmoid * (1.0 + gate * (1.0 - gate_sigmoid))
    ).astype(BF)
    up_grad_low = (activation_grad * swish).astype(BF)
    hidden_grads = jnp.concatenate([gate_grad_low, up_grad_low], axis=1)
    normed2_grad = scatter_rows(times_transposed(hidden_grads, gate_up))
    branch_two = scatter_rows(times_transposed(activation_low, down_all))
    own_output = (mixed + branch_two).astype(BF)
    output = pair_rows(own_output).reshape(tokens.shape)
    gate_up_sums = scatter_gradient(normed2_all, hidden_grads)
    down_sums = scatter_gradient(cotangent_all, activation_low)

    mixed_grad = own_cotangent.astype(F32) + norm_back(normed2_grad, unit2, inverse2, second_gain)
    mixed_grad_all = gather_rows(mixed_grad.astype(BF))
    attended_grad = times(mixed_grad_all, out_all).astype(BF).reshape(heads_shape)
    out_sums = scatter_gradient(mixed_grad_all, attended_low)
    delta = jnp.sum(attended_grad.astype(F32) * attended, axis=-1)
    probs = jnp.where(allowed, jnp.exp(masked - log_total), 0.0)
    prob_grad = jnp.einsum("qhd,khd->hqk", attended_grad, value_low, preferred_element_type=F32)
    score_grad = (probs * (prob_grad - delta.T[..., None])).astype(BF)
    query_grad = jnp.einsum("hqk,khd->qhd", score_grad, key_low, preferred_element_type=F32)
    key_grad = jnp.einsum("hqk,qhd->khd", score_grad, query_low, preferred_element_type=F32)
    value_grad = jnp.einsum("hqk,qhd->khd", probs.astype(BF), attended_grad, preferred_element_type=F32)
    value_grad_low = value_grad.astype(BF).reshape(length, columns)
    key_turned = rotate_back(rounded(key_grad * score_scale), cosine, sine, rotary)
    key_bias_part = jnp.sum(key_turned[..., :rotary], axis=0)
    key_grad_low = key_turned.astype(BF).reshape(length, columns)
    query_grad_low = (
        rotate_back(rounded(query_grad * score_scale), cosine, sine, rotary)
        .astype(BF)
        .reshape(length, columns)
    )
    projection_grads = jnp.concatenate([query_grad_low, key_grad_low, value_grad_low], axis=1)
    normed1_grad = scatter_rows(times_transposed(projection_grads, projections))
    projection_sums = scatter_gradient(normed1_all, projection_grads)
    own_gradient = (mixed_grad + norm_back(normed1_grad, unit1, inverse1, first_gain)).astype(BF)
    tokens_gradient = pair_rows(own_gradient).reshape(tokens.shape)

    def placed(values, first, count):
        return lax.dynamic_update_slice_in_dim(jnp.zeros((count,), F32), values, first, 0)

    small = jnp.concatenate(
        [
            jnp.sum(normed1_grad * unit1, axis=0),
            jnp.sum(normed1_grad, axis=0),
            jnp.sum(normed2_grad * unit2, axis=0),
            jnp.sum(normed2_grad, axis=0),
            placed(jnp.sum(query_grad_low.astype(F32), axis=0), first_col, model_width),
            placed(jnp.sum(value_grad_low.astype(F32), axis=0), first_col, model_width),
            placed(key_bias_part.reshape(-1), first_head * rotary, HEADS * rotary),
        ]
    )
    small = total(small.reshape(-1, 128), ("tp", "fsdp", "ctx")).reshape(-1)
    parts = [small[i * model_width : (i + 1) * model_width] for i in range(6)]
    key_bias_sum = small[6 * model_width :].reshape(HEADS, rotary)

    def joined(sums, first, last):
        return sums[:, :, first:last].astype(F32).reshape(weight_rows, -1)

    return (
        output,
        tokens_gradient,
        parts[0],
        parts[1],
        joined(projection_sums, 0, columns),
        parts[4],
        joined(projection_sums, columns, 2 * columns),
        key_bias_sum,
        joined(projection_sums, 2 * columns, 3 * columns),
        parts[5],
        joined(out_sums, 0, columns).T,
        parts[2],
        parts[3],
        joined(gate_up_sums, 0, hidden),
        joined(gate_up_sums, hidden, 2 * hidden),
        joined(down_sums, 0, hidden).T,
    )


def solution(mesh):
    placed = (
        P("fsdp", "ctx", None),
        P("fsdp", "ctx"),
        P("fsdp", "ctx"),
        P(),
        P(),
        P(("fsdp", "ctx"), "tp"),
        P(),
        P(("fsdp", "ctx"), "tp"),
        P(),
        P(("fsdp", "ctx"), "tp"),
        P(),
        P("tp", ("fsdp", "ctx")),
        P(),
        P(),
        P(("fsdp", "ctx"), "tp"),
        P(("fsdp", "ctx"), "tp"),
        P("tp", ("fsdp", "ctx")),
        P("fsdp", "ctx", None),
    )
    return jax.shard_map(
        on_device,
        mesh=mesh,
        in_specs=placed,
        out_specs=(
            P("fsdp", "ctx", None),
            P("fsdp", "ctx", None),
            P(),
            P(),
            P(("fsdp", "ctx"), "tp"),
            P(),
            P(("fsdp", "ctx"), "tp"),
            P(),
            P(("fsdp", "ctx"), "tp"),
            P(),
            P("tp", ("fsdp", "ctx")),
            P(),
            P(),
            P(("fsdp", "ctx"), "tp"),
            P(("fsdp", "ctx"), "tp"),
            P("tp", ("fsdp", "ctx")),
        ),
        check_vma=False,
    )
```

```python
import math

import jax
import jax.numpy as jnp
from jax import lax
from jax.experimental import pallas as pl
from jax.experimental.pallas import tpu as pltpu
from jax.sharding import PartitionSpec as P

HEADS = 32
HEAD = 64
ROTARY = 16


NEG = -1e30
EPS = 1e-05
BF = jnp.bfloat16
F32 = jnp.float32


def norm_parts(values, gain, shift):
    mean = jnp.mean(values, axis=-1, keepdims=True)
    centred = values - mean
    inverse = lax.rsqrt(jnp.mean(centred * centred, axis=-1, keepdims=True) + EPS)
    unit = centred * inverse
    return (unit * gain + shift, unit, inverse)


def norm_back(grad, unit, inverse, gain):
    scaled = grad * gain
    return inverse * (
        scaled
        - jnp.mean(scaled, axis=-1, keepdims=True)
        - unit * jnp.mean(scaled * unit, axis=-1, keepdims=True)
    )


def dot(left, right, dims, out=F32):
    return lax.dot_general(left, right, ((dims[:1], dims[1:]), ((), ())), preferred_element_type=out)


def contract_rows(left, right, out=F32):
    return dot(left, right, (0, 0), out)


def times(left, right, out=F32):
    return dot(left, right, (1, 0), out)


def times_transposed(left, right, out=F32):
    return dot(left, right, (1, 1), out)


def after(values, *others):
    return lax.optimization_barrier((values,) + others)[0]


def shift(values, axis, step):
    size = lax.axis_size(axis)
    return lax.ppermute(values, axis, [(i, (i + step) % size) for i in range(size)])


def swap(values, axis, bit):
    size = lax.axis_size(axis)
    return lax.ppermute(values, axis, [(i, i ^ bit) for i in range(size)])


def arrival(size):
    order = [0]
    for step in range(1, (size - 1) // 2 + 1):
        order += [-step, step]
    if size % 2 == 0:
        order.append(size // 2)
    return order


def arrived(whole):
    me, size = lax.axis_index("ctx"), lax.axis_size("ctx")
    rows = whole.shape[0] // size
    return jnp.concatenate(
        [
            lax.dynamic_slice_in_dim(whole, (me + step) % size * rows, rows, 0)
            for step in arrival(size)
        ],
        0,
    )


def in_order(blocks):
    me, size = lax.axis_index("ctx"), lax.axis_size("ctx")
    spots = {step % size: i for i, step in enumerate(arrival(size))}
    ring = jnp.concatenate([blocks[spots[k % size]] for k in range(2 * size)], 0)
    rows = blocks[0].shape[0]
    return lax.dynamic_slice_in_dim(ring, (size - me) % size * rows, size * rows, 0)


def line_gather(block, axis):
    size = lax.axis_size(axis)
    blocks = [block]
    right = left = block
    for _ in range((size - 1) // 2):
        right = shift(right, axis, 1)
        left = shift(left, axis, -1)
        blocks += [right, left]
    if size % 2 == 0:
        half = block.shape[0] // 2
        blocks += [shift(right[:half], axis, 1), shift(left[half:], axis, -1)]
    return jnp.concatenate(blocks, 0), (right, left)


def line_sum(blocks, axis):
    size = lax.axis_size(axis)
    half = blocks[0].shape[0] // 2
    right = left = first = None
    if size % 2 == 0:
        far = blocks[-1].astype(BF)
        right = shift(far[:half], axis, 1)
        left = shift(far[half:], axis, -1)
    for step in range((size - 1) // 2, 0, -1):
        ahead, behind = blocks[2 * step], blocks[2 * step - 1]
        if right is not None:
            if right.shape[0] == half:
                first = (right, left)
                ahead = jnp.concatenate([ahead[:half] + right.astype(F32), ahead[half:]], 0)
                behind = jnp.concatenate([behind[:half], behind[half:] + left.astype(F32)], 0)
            else:
                ahead = ahead + right.astype(F32)
                behind = behind + left.astype(F32)
        right = shift(ahead.astype(BF), axis, 1)
        left = shift(behind.astype(BF), axis, -1)
    return blocks[0] + right.astype(F32) + left.astype(F32), first


def plane_gather(block, axis, *tokens):
    half = block.shape[0] // 2
    near = swap(block, axis, 1)
    side = swap(block, axis, 2)
    near, side = after((near, side), *tokens)
    low = swap(near[:half], axis, 2)
    high = swap(side[half:], axis, 1)
    return [block, near, side, low, high]


def total(values, axes):
    for axis in axes:
        bit = 1
        while bit < lax.axis_size(axis):
            values = values + swap(values, axis, bit)
            bit *= 2
    return values


def near_first(values, width):
    me = lax.axis_index("fsdp")
    last = values.ndim - 1
    return jnp.concatenate(
        [
            lax.dynamic_slice_in_dim(values, (me ^ i) * width, width, last)
            for i in range(lax.axis_size("fsdp"))
        ],
        last,
    )


def both_cores(block):
    me = lax.axis_index("tp")
    other = swap(block, "tp", 1)
    return jnp.concatenate([jnp.where(me == 0, block, other), jnp.where(me == 0, other, block)], 0)


def gather_rows(block):
    lined, first = line_gather(block, "ctx")
    return jnp.concatenate([lined, swap(lined, "tp", 1)], 0), first, lined


def scatter_parts(left, right):
    half = left.shape[0] // 2
    size = lax.axis_size("ctx")
    rows = half // size
    other = swap(times_transposed(left[half:], right).astype(BF), "tp", 1)
    own = times_transposed(left[:half], right)
    return [
        own[i * rows : (i + 1) * rows] + other[i * rows : (i + 1) * rows].astype(F32)
        for i in range(size)
    ], other


ANY = pl.BlockSpec(memory_space=pl.ANY)
WHOLE = pl.BlockSpec(memory_space=pltpu.VMEM)
SCALARS = pl.BlockSpec(memory_space=pltpu.SMEM)


def params(megabytes=32):
    return pltpu.CompilerParams(vmem_limit_bytes=megabytes * 2**20)


def ctx_index():
    return lax.axis_index("ctx").astype(jnp.int32).reshape(1)


def pack(straight, turned):
    size = lax.axis_size("ctx")
    rows = (straight[0].shape[0] if straight else turned[0].shape[1])
    widths = [a.shape[1] // size for a in straight] + [a.shape[0] // size for a in turned]

    def kernel(*refs):
        out = refs[-1]
        for j in range(size):
            first = 0
            for i, width in enumerate(widths):
                if i < len(straight):
                    block = refs[i][:, j * width : (j + 1) * width]
                else:
                    block = refs[i][j * width : (j + 1) * width, :].T
                out[j, :, first : first + width] = block
                first += width

    return pl.pallas_call(
        kernel,
        out_shape=jax.ShapeDtypeStruct((size, rows, sum(widths)), BF),
        in_specs=[WHOLE] * (len(straight) + len(turned)),
        out_specs=WHOLE,
        compiler_params=params(),
        name="pack",
    )(*straight, *turned)


def unpack(whole, straight, turned):
    size, rows = whole.shape[:2]
    widths = straight + turned

    def kernel(held, *outs):
        for j in range(size):
            first = 0
            for i, width in enumerate(widths):
                block = held[j, :, first : first + width].astype(F32)
                if i < len(straight):
                    outs[i][:, j * width : (j + 1) * width] = block
                else:
                    outs[i][j * width : (j + 1) * width, :] = block.T
                first += width

    return pl.pallas_call(
        kernel,
        out_shape=[jax.ShapeDtypeStruct((rows, size * w), F32) for w in straight]
        + [jax.ShapeDtypeStruct((size * w, rows), F32) for w in turned],
        in_specs=[WHOLE],
        out_specs=[WHOLE] * len(widths),
        compiler_params=params(),
        name="unpack",
    )(whole)


def turned_by(values, cosine, low, high, sign):
    step = ROTARY // 2
    ahead = jnp.concatenate([values[:, step:], values[:, :step]], 1)
    behind = jnp.concatenate([values[:, -step:], values[:, :-step]], 1)
    return values * cosine + sign * (ahead * low + behind * high)


def allowed_keys(start_ref, first, rows, keys):
    key = lax.broadcasted_iota(jnp.int32, (rows, keys), 1)
    query = lax.broadcasted_iota(jnp.int32, (rows, keys), 0) + first
    return (key >= start_ref[pl.ds(first, rows), :]) & (key <= query)


def attend(order, projected, bias, cosine, low, high, starts, rows):
    length, columns = projected.shape[0], projected.shape[1] // 3
    width = cosine.shape[1]
    block = 2 * rows
    scale = 1.0 / math.sqrt(HEAD)

    def kernel(order_ref, pre, bias_ref, cos_ref, low_ref, high_ref, start_ref, out, held, exact, logs):
        def lay(b, carry):
            at = pl.ds(pl.multiple_of(order_ref[b], rows), rows)
            to = pl.ds(pl.multiple_of(b * rows, rows), rows)
            values = pre[at, :] + bias_ref[...]
            tables = (cos_ref[to, :], low_ref[to, :], high_ref[to, :])
            for first in range(0, 2 * columns, width):
                part = turned_by(values[:, first : first + width], *tables, 1.0)
                held[to, first : first + width] = part.astype(BF)
            held[to, 2 * columns :] = values[:, 2 * columns :].astype(BF)
            return carry

        lax.fori_loop(0, length // rows, lay, 0)
        for first in range(0, columns, width):
            for start in range(0, length, block):
                keys = start + block
                allowed = allowed_keys(start_ref, start, block, keys)
                parts = []
                for head in range(first, first + width, HEAD):
                    query = held[start:keys, head : head + HEAD]
                    key = held[:keys, columns + head : columns + head + HEAD]
                    value = held[:keys, 2 * columns + head : 2 * columns + head + HEAD]
                    scores = jnp.where(allowed, times_transposed(query, key) * scale, NEG)
                    highest = jnp.max(scores, axis=1, keepdims=True)
                    weights = jnp.exp(scores - highest)
                    sums = jnp.sum(weights, axis=1, keepdims=True)
                    parts.append(times(weights.astype(BF), value) / sums)
                    logs[start:keys, head // HEAD : head // HEAD + 1] = highest + jnp.log(sums)
                both = parts[0] if len(parts) == 1 else jnp.concatenate(parts, 1)
                exact[start:keys, first : first + width] = both
                for b in range(2):
                    at = pl.ds(pl.multiple_of(order_ref[start // rows + b], rows), rows)
                    out[at, first : first + width] = both[b * rows : (b + 1) * rows].astype(BF)

    return pl.pallas_call(
        kernel,
        out_shape=[
            jax.ShapeDtypeStruct((length, columns), BF),
            jax.ShapeDtypeStruct((length, 3 * columns), BF),
            jax.ShapeDtypeStruct((length, columns), F32),
            jax.ShapeDtypeStruct((length, columns // HEAD), F32),
        ],
        in_specs=[SCALARS] + [WHOLE] * 6,
        out_specs=[WHOLE] * 4,
        compiler_params=params(56),
        name="attend",
    )(order, projected, bias, cosine, low, high, starts)


def attend_back(order, grad, held, exact, logs, cosine, low, high, starts, rows):
    length, columns = exact.shape
    width = cosine.shape[1]
    block = 2 * rows
    scale = 1.0 / math.sqrt(HEAD)

    def kernel(
        order_ref, grad_ref, kept, exact_ref, logs_ref, cos_ref, low_ref, high_ref, start_ref, out, sums, grads, keyed, valued
    ):
        def lay(b, carry):
            at = pl.ds(pl.multiple_of(order_ref[b], rows), rows)
            grads[pl.ds(pl.multiple_of(b * rows, rows), rows), :] = grad_ref[at, :]
            return carry

        lax.fori_loop(0, length // rows, lay, 0)
        sums[...] = jnp.zeros_like(sums)

        def turn_back(values, start, count):
            at = slice(start, start + count)
            return turned_by(values, cos_ref[at, :], low_ref[at, :], high_ref[at, :], -1.0)

        def put(values, start, first):
            for b in range(values.shape[0] // rows):
                at = pl.ds(pl.multiple_of(order_ref[start // rows + b], rows), rows)
                out[at, first : first + width] = values[b * rows : (b + 1) * rows]

        for first in range(0, columns, width):
            keyed[...] = jnp.zeros_like(keyed)
            valued[...] = jnp.zeros_like(valued)
            for start in range(0, length, block):
                keys = start + block
                allowed = allowed_keys(start_ref, start, block, keys)
                parts = []
                for head in range(first, first + width, HEAD):
                    lanes = slice(head - first, head - first + HEAD)
                    query = kept[start:keys, head : head + HEAD]
                    key = kept[:keys, columns + head : columns + head + HEAD]
                    value = kept[:keys, 2 * columns + head : 2 * columns + head + HEAD]
                    upper = grads[start:keys, head : head + HEAD]
                    delta = jnp.sum(
                        upper.astype(F32) * exact_ref[start:keys, head : head + HEAD],
                        axis=1,
                        keepdims=True,
                    )
                    scores = times_transposed(query, key) * scale
                    log_total = logs_ref[start:keys, head // HEAD : head // HEAD + 1]
                    probs = jnp.where(allowed, jnp.exp(jnp.where(allowed, scores, NEG) - log_total), 0.0)
                    slope = (probs * (times_transposed(upper, value) - delta)).astype(BF)
                    parts.append(times(slope, key) * scale)
                    keyed[:keys, lanes] += contract_rows(slope, query)
                    valued[:keys, lanes] += contract_rows(probs.astype(BF), upper)
                both = parts[0] if len(parts) == 1 else jnp.concatenate(parts, 1)
                turned = turn_back(both.astype(BF).astype(F32), start, block).astype(BF)
                put(turned, start, first)
                sums[0:1, first : first + width] += jnp.sum(turned.astype(F32), axis=0, keepdims=True)
            for start in range(0, length, block):
                at = slice(start, start + block)
                turned = turn_back((keyed[at, :] * scale).astype(BF).astype(F32), start, block)
                put(turned.astype(BF), start, columns + first)
                sums[0:1, columns + first : columns + first + width] += jnp.sum(turned, axis=0, keepdims=True)
                lowered = valued[at, :].astype(BF)
                put(lowered, start, 2 * columns + first)
                sums[0:1, 2 * columns + first : 2 * columns + first + width] += jnp.sum(
                    lowered.astype(F32), axis=0, keepdims=True
                )

    return pl.pallas_call(
        kernel,
        out_shape=[
            jax.ShapeDtypeStruct((length, 3 * columns), BF),
            jax.ShapeDtypeStruct((8, 3 * columns), F32),
        ],
        in_specs=[SCALARS] + [WHOLE] * 8,
        out_specs=[WHOLE] * 2,
        scratch_shapes=[
            pltpu.VMEM((length, columns), BF),
            pltpu.VMEM((length, width), F32),
            pltpu.VMEM((length, width), F32),
        ],
        compiler_params=params(56),
        name="attend_back",
    )(order, grad, held, exact, logs, cosine, low, high, starts)


def exchange(blocks):
    return lax.all_to_all(blocks, "ctx", 0, 0)


def rows_product(pairs):
    length, height = pairs[0][0].shape
    widths = [grads.shape[1] for _, grads in pairs]
    tile = 256

    def kernel(*refs):
        out, first = refs[-1], 0
        for i, width in enumerate(widths):
            out[:, first : first + width] = contract_rows(refs[2 * i][...], refs[2 * i + 1][...]).astype(BF)
            first += width

    specs = []
    for width in widths:
        specs += [
            pl.BlockSpec((length, tile), lambda i: (0, i)),
            pl.BlockSpec((length, width), lambda i: (0, 0)),
        ]
    return pl.pallas_call(
        kernel,
        grid=(height // tile,),
        out_shape=jax.ShapeDtypeStruct((height, sum(widths)), BF),
        in_specs=specs,
        out_specs=pl.BlockSpec((tile, sum(widths)), lambda i: (i, 0)),
        compiler_params=params(48),
        cost_estimate=pl.CostEstimate(flops=1, bytes_accessed=1, transcendentals=0),
        name="rows_product",
    )(*[array for pair in pairs for array in pair])


def joined(pieces, first=None, last=None):
    return jnp.concatenate([piece[:, first:last] for piece in pieces], 0)


def scatter_gradient(pairs, tokens, axis="fsdp"):
    width = pairs[0][0].shape[1] // lax.axis_size(axis)

    def block(i):
        return jnp.concatenate(
            [contract_rows(rows_in[:, i * width : (i + 1) * width], grads) for rows_in, grads in pairs], 1
        )

    far = block(3).astype(BF)
    half = width // 2
    low = swap(far[:half], axis, 1)
    high = swap(far[half:], axis, 2)
    side, near, own = block(2), block(1), block(0)
    low, high = after((low, high), *tokens[0])
    side = jnp.concatenate([side[:half] + low.astype(F32), side[half:]], 0).astype(BF)
    near = jnp.concatenate([near[:half], near[half:] + high.astype(F32)], 0).astype(BF)
    side, near = swap(side, axis, 2), swap(near, axis, 1)
    side, near = after((side, near), *tokens[1])
    return (own + side.astype(F32) + near.astype(F32)).astype(BF)


def on_device(
    tokens,
    segments,
    positions,
    first_gain,
    first_shift,
    query_weight,
    query_bias,
    key_weight,
    key_bias,
    value_weight,
    value_bias,
    out_weight,
    second_gain,
    second_shift,
    gate_weight,
    up_weight,
    down_weight,
    cotangent,
):
    local_rows, model_width = tokens.shape[1:]
    tensor_rank, tensor_size = lax.axis_index("tp"), lax.axis_size("tp")
    ctx_rank, ctx_size = lax.axis_index("ctx"), lax.axis_size("ctx")
    length = local_rows * ctx_size
    own_rows = local_rows // tensor_size
    heads = HEADS // (tensor_size * ctx_size)
    columns = heads * HEAD
    first_head = (tensor_rank * ctx_size + ctx_rank) * heads
    first_col = first_head * HEAD
    hidden = gate_weight.shape[1] // ctx_size
    width = model_width // lax.axis_size("fsdp")

    def own(values):
        return lax.dynamic_slice_in_dim(values[0], tensor_rank * own_rows, own_rows, 0)

    inputs = own(tokens).astype(F32)
    own_cotangent = own(cotangent)
    normed1, unit1, inverse1 = norm_parts(inputs, first_gain, first_shift)
    segment_blocks = [shift(segments, "ctx", k) for k in range(1, ctx_size)]
    packed = pack([query_weight, key_weight, value_weight], [out_weight])
    attention = exchange(after(packed, *segment_blocks))
    attention = attention.reshape(-1, 4 * columns)
    normed1_all, first1, lined1 = gather_rows(near_first(normed1.astype(BF), width))
    pieces = plane_gather(attention, "fsdp", *first1)
    projections = joined(pieces, 0, 3 * columns)
    out_all = joined(pieces, 3 * columns, 4 * columns)

    ctx_places = jnp.arange(ctx_size, dtype=jnp.int32)
    starts = jnp.where((ctx_places == ctx_rank)[:, None], segments, 0)
    for k, block in enumerate(segment_blocks, 1):
        starts = jnp.where((ctx_places == (ctx_rank - k) % ctx_size)[:, None], block, starts)
    starts = starts.reshape(length, 1)
    ahead = (ctx_places - ctx_rank) % ctx_size
    spot = jnp.zeros((ctx_size,), jnp.int32)
    for i, step in enumerate(arrival(ctx_size)):
        spot = jnp.where(ahead == step % ctx_size, i, spot)
    core = (jnp.arange(tensor_size, dtype=jnp.int32) != tensor_rank).astype(jnp.int32)
    order = ((core[None, :] * ctx_size + spot[:, None]) * own_rows).reshape(-1)
    lane = jnp.arange(min(columns, 128), dtype=jnp.int32) % HEAD
    half = ROTARY // 2
    freqs = 1.0 / 10000.0 ** ((lane % half).astype(F32) * 2.0 / ROTARY)
    places = (jnp.arange(length, dtype=jnp.int32)[:, None] - starts).astype(F32)
    angle = places * jnp.where(lane < ROTARY, freqs, 0.0)
    cosine, sine = jnp.cos(angle), jnp.sin(angle)
    low = jnp.where(lane < half, -sine, 0.0)
    high = jnp.where((lane >= half) & (lane < ROTARY), sine, 0.0)

    bias = jnp.concatenate(
        [
            lax.dynamic_slice_in_dim(query_bias, first_col, columns, 0),
            jnp.pad(
                lax.dynamic_slice_in_dim(key_bias, first_head, heads, 0), ((0, 0), (0, HEAD - ROTARY))
            ).reshape(-1),
            lax.dynamic_slice_in_dim(value_bias, first_col, columns, 0),
        ]
    ).reshape(1, -1)
    projected = times(normed1_all, projections)
    attended, held, exact, logs = attend(
        order, projected, bias, cosine, low, high, starts, own_rows
    )
    entering = exchange(after(pack([gate_weight, up_weight], [down_weight]), lined1))
    cotangent_all, cotangent_first, _ = gather_rows(after(own_cotangent, lined1))
    parts, _ = scatter_parts(attended, out_all)
    attended_sum, _ = line_sum(after(parts, entering, *cotangent_first), "ctx")
    entering = entering.reshape(-1, 3 * hidden)
    entered = lax.all_gather(entering, "fsdp", axis=0, tiled=True)
    mixed = inputs + near_first(attended_sum, width)
    normed2, unit2, inverse2 = norm_parts(mixed, second_gain, second_shift)
    normed2_all, _, _ = gather_rows(normed2.astype(BF))
    gate_up, down_all = entered[:, : 2 * hidden], entered[:, 2 * hidden :]

    gate_upward = times(normed2_all, gate_up)
    gate, upward = gate_upward[:, :hidden], gate_upward[:, hidden:]
    gate_sigmoid = jax.nn.sigmoid(gate)
    swish = gate * gate_sigmoid
    activation_low = (swish * upward).astype(BF)
    activation_grad = times(cotangent_all, down_all)
    gate_grad_low = (
        activation_grad * upward * gate_sigmoid * (1.0 + gate * (1.0 - gate_sigmoid))
    ).astype(BF)
    up_grad_low = (activation_grad * swish).astype(BF)
    hidden_grads = jnp.concatenate([gate_grad_low, up_grad_low], axis=1)
    parts, _ = scatter_parts(hidden_grads, gate_up)
    normed2_grad, first4 = line_sum(parts, "ctx")
    activation_low, hidden_low = after((activation_low, hidden_grads), *first4)
    hidden_sums = lax.psum_scatter(
        rows_product([(normed2_all, hidden_low), (cotangent_all, activation_low)]),
        "fsdp",
        scatter_dimension=0,
        tiled=True,
    )
    mixed_grad = own_cotangent.astype(F32) + norm_back(normed2_grad, unit2, inverse2, second_gain)
    mixed_grad_all, _, lined3 = gather_rows(near_first(mixed_grad.astype(BF), width))
    parts, _ = scatter_parts(activation_low, down_all)
    branch_two, _ = line_sum(after(parts, lined3), "ctx")
    attended_grad = times(mixed_grad_all, out_all).astype(BF)
    projection_grads, bias_sums = attend_back(
        order, attended_grad, held, exact, logs, cosine, low, high, starts, own_rows
    )
    hidden_back = exchange(hidden_sums.reshape(ctx_size, -1, 3 * hidden))
    projection_grads = after(projection_grads, branch_two)
    parts, other = scatter_parts(projection_grads, projections)
    normed1_grad, first6 = line_sum(parts, "ctx")
    gate_sum, up_sum, down_sum = unpack(after(hidden_back, *first6), [hidden, hidden], [hidden])
    projection_grads = after(projection_grads, other)
    attention_sums = scatter_gradient(
        [(normed1_all, projection_grads), (mixed_grad_all, attended)], ((), ())
    )
    attention_back = exchange(attention_sums.reshape(ctx_size, -1, 4 * columns))
    query_sum, key_sum, value_sum, out_sum = unpack(attention_back, [columns] * 3, [columns])
    output = both_cores((mixed + branch_two).astype(BF)).reshape(tokens.shape)
    normed1_grad = near_first(normed1_grad, width)
    own_gradient = (mixed_grad + norm_back(normed1_grad, unit1, inverse1, first_gain)).astype(BF)
    tokens_gradient = both_cores(own_gradient).reshape(tokens.shape)

    def placed(values, first, count):
        return lax.dynamic_update_slice_in_dim(jnp.zeros((count,), F32), values, first, 0)

    vectors = [
        jnp.sum(normed1_grad * unit1, axis=0),
        jnp.sum(normed1_grad, axis=0),
        jnp.sum(normed2_grad * unit2, axis=0),
        jnp.sum(normed2_grad, axis=0),
    ]
    key_bias_part = bias_sums[0, columns : 2 * columns].reshape(heads, HEAD)[:, :ROTARY]
    small = jnp.concatenate(
        [
            *vectors,
            placed(bias_sums[0, :columns], first_col, model_width),
            placed(bias_sums[0, 2 * columns :], first_col, model_width),
            placed(key_bias_part.reshape(-1), first_head * ROTARY, HEADS * ROTARY),
        ]
    )
    small = total(small.reshape(-1, 128), ("tp", "fsdp", "ctx")).reshape(-1)
    parts = [small[i * model_width : (i + 1) * model_width] for i in range(6)]
    key_bias_sum = small[6 * model_width :].reshape(HEADS, ROTARY)

    return (
        output,
        tokens_gradient,
        parts[0],
        parts[1],
        query_sum,
        parts[4],
        key_sum,
        key_bias_sum,
        value_sum,
        parts[5],
        out_sum,
        parts[2],
        parts[3],
        gate_sum,
        up_sum,
        down_sum,
    )


def solution(mesh):
    placed = (
        P("fsdp", "ctx", None),
        P("fsdp", "ctx"),
        P("fsdp", "ctx"),
        P(),
        P(),
        P(("fsdp", "ctx"), "tp"),
        P(),
        P(("fsdp", "ctx"), "tp"),
        P(),
        P(("fsdp", "ctx"), "tp"),
        P(),
        P("tp", ("fsdp", "ctx")),
        P(),
        P(),
        P(("fsdp", "ctx"), "tp"),
        P(("fsdp", "ctx"), "tp"),
        P("tp", ("fsdp", "ctx")),
        P("fsdp", "ctx", None),
    )
    return jax.shard_map(
        on_device,
        mesh=mesh,
        in_specs=placed,
        out_specs=(
            P("fsdp", "ctx", None),
            P("fsdp", "ctx", None),
            P(),
            P(),
            P(("fsdp", "ctx"), "tp"),
            P(),
            P(("fsdp", "ctx"), "tp"),
            P(),
            P(("fsdp", "ctx"), "tp"),
            P(),
            P("tp", ("fsdp", "ctx")),
            P(),
            P(),
            P(("fsdp", "ctx"), "tp"),
            P(("fsdp", "ctx"), "tp"),
            P("tp", ("fsdp", "ctx")),
        ),
        check_vma=False,
    )
```
